256 devices in a mesh: energy: 128 (over y, z_lo, x, core), slab: 2 (over z_hi).
Axes of the slice: x: 4, y: 4, z: 8 (z_hi: 2, z_lo: 4; z = z_hi * 4 + z_lo), core: 2. Of those that a mesh axis runs over, the one named last changes fastest.
Arguments:
- green_ret: bfloat16 [384, 4, 3, 2, 192, 192], P('energy', 'slab'), may hold values from -0.3125 to 0.3125
- sigma_less: bfloat16 [384, 4, 2, 192, 192], P('energy', 'slab'), may hold values from -6 to 6
- screened: float32 [384, 4, 2, 36864], P(None, 'slab', None, 'energy'), may hold values from -4 to 4
Outputs:
- sigma_new: bfloat16 [384, 4, 2, 192, 192], P('energy', 'slab')
- renewed: bfloat16 [384, 4, 2, 192, 192], P('energy', 'slab')
The draws below stay inside these ranges and needn't reach their ends.
All inputs are finite; a program needn't handle non-finite values.
Results may differ from the reference program's by a relative error of at most 0.0085.
Values may be sent and summed in bfloat16 or wider, within the bound.
A program may use at most 128 MiB of HBM per device.

```python
import math
import jax
import jax.numpy as jnp
from jax import lax

B = 192
E = 384
S = 4


def block_levels(key, dims, split, low, high):
    gain, own = 1.0, jax.random.fold_in(key, 6)
    for axis_at, blocks in split:
        draws = jnp.exp(jax.random.uniform(jax.random.fold_in(own, axis_at), (blocks,), jnp.float32, low / len(split), high / len(split)))
        gain = gain * jnp.repeat(draws, dims[axis_at] // blocks).reshape([-1 if axis == axis_at else 1 for axis in range(len(dims))])
    return gain


def scatter_about(key, extent, spread, reach, split=(), held_as=jnp.bfloat16):
    level = block_levels(key, extent, split, -0.22, 0.18) if split else 1.0
    entries = jax.random.normal(key, extent, jnp.float32) * spread * level
    return jnp.minimum(jnp.maximum(entries, -reach), reach).astype(held_as)


def setup_inputs(seed: int = 0) -> dict:
    streams_of = jax.random.split(jax.random.key(seed), 4)
    green_ret = scatter_about(streams_of[0], (E, S, 3, 2, B, B), (2 * B) ** -0.5, 0.3125, ((0, 128), (1, 2)))
    sigma_less = scatter_about(streams_of[1], (E, S, 2, B, B), 1.0, 6.0, ((0, 128), (1, 2)))
    screened = scatter_about(streams_of[2], (E, S, 2, B * B), 0.5, 4.0, ((1, 2), (3, 128)), jnp.float32)
    return dict(green_ret=green_ret, sigma_less=sigma_less, screened=screened)


def cmul_adj(left, right):
    lr = left[..., 0, :, :].astype(jnp.float32)
    li = left[..., 1, :, :].astype(jnp.float32)
    rr = right[..., 0, :, :].astype(jnp.float32)
    ri = right[..., 1, :, :].astype(jnp.float32)
    real = jnp.einsum('...ab,...cb->...ac', lr, rr) + jnp.einsum('...ab,...cb->...ac', li, ri)
    imag = jnp.einsum('...ab,...cb->...ac', li, rr) - jnp.einsum('...ab,...cb->...ac', lr, ri)
    return jnp.stack([real, imag], axis=-3)

def cmul_plain(left, right):
    lr = left[..., 0, :, :].astype(jnp.float32)
    li = left[..., 1, :, :].astype(jnp.float32)
    rr = right[..., 0, :, :].astype(jnp.float32)
    ri = right[..., 1, :, :].astype(jnp.float32)
    real = jnp.einsum('...ab,...bc->...ac', lr, rr) - jnp.einsum('...ab,...bc->...ac', li, ri)
    imag = jnp.einsum('...ab,...bc->...ac', lr, ri) + jnp.einsum('...ab,...bc->...ac', li, rr)
    return jnp.stack([real, imag], axis=-3)

def reference(green_ret, sigma_less, screened):

    def congruence(pair):
        blocks, sigma = pair
        padded = jnp.pad(sigma, ((1, 1), (0, 0), (0, 0), (0, 0)))
        total = jnp.zeros(sigma.shape, jnp.float32)
        for k in range(3):
            coupling = blocks[:, k]
            inner = cmul_adj(padded[k:k + S], coupling).astype(jnp.bfloat16)
            total = total + cmul_plain(coupling, inner)
        return total.astype(jnp.bfloat16)
    lesser = lax.map(congruence, (green_ret, sigma_less))
    flat = lesser.astype(jnp.float32).reshape(E, S, 2, B * B)
    gcomp = flat[:, :, 0] + 1j * flat[:, :, 1]
    wcomp = screened[:, :, 0] + 1j * screened[:, :, 1]
    conv = jnp.fft.ifft(jnp.fft.fft(gcomp, axis=0) * jnp.fft.fft(wcomp, axis=0), axis=0) / math.sqrt(E)
    sigma_new = jnp.stack([conv.real, conv.imag], axis=2).reshape(E, S, 2, B, B).astype(jnp.bfloat16)

    def second(pair):
        blocks, fresh = pair
        diag = blocks[:, 1]
        inner = cmul_adj(fresh, diag).astype(jnp.bfloat16)
        return cmul_plain(diag, inner).astype(jnp.bfloat16)
    renewed = lax.map(second, (green_ret, sigma_new))
    return (sigma_new, renewed)
```

```python
import functools
import math

import jax
import jax.numpy as jnp
import numpy as np
from jax import lax
from jax.experimental import pallas as pl
from jax.experimental.pallas import tpu as pltpu
from jax.sharding import PartitionSpec as P

MESH = pl.DeviceIdType.MESH
F32, BF16 = jnp.float32, jnp.bfloat16
E, B = 384, 192
CHIPS, PER_CHIP, OWN = 64, 6, 3
ROWS, PITCH = 54, 56
HALF = B * 3 // 2
SCALE = 1.0 / (E * math.sqrt(E))


def tables():
    point = np.arange(E)
    held = np.array([PER_CHIP * c + k for k in range(PER_CHIP) for c in range(CHIPS)])

    def parts(rows, cols):
        angle = (rows[:, None] * cols[None, :] % E) * (2.0 * np.pi / E)
        return np.cos(angle), np.sin(angle)

    cos, sin = parts(point, point)
    whole = np.concatenate([np.concatenate([cos, sin], 1), np.concatenate([-sin, cos], 1)], 0)
    there = np.concatenate(parts(point, held), 1)
    back = np.concatenate(parts(held, point), 1)
    return [t.astype(np.float32).astype(BF16) for t in (whole, there, back)]


def nn(a, b):
    return lax.dot_general(a, b, (((1,), (0,)), ((), ())), preferred_element_type=F32)


def nt(a, b):
    return lax.dot_general(a, b, (((1,), (1,)), ((), ())), preferred_element_type=F32)


def adjoint_product(ar, ai, br, bi):
    return (nt(ar, br) + nt(ai, bi)).astype(BF16), (nt(ai, br) - nt(ar, bi)).astype(BF16)


def product(ar, ai, br, bi):
    return nn(ar, br) - nn(ai, bi), nn(ar, bi) + nn(ai, br)


def unpack(row):
    return (
        jnp.concatenate([row[:, :128], row[:, 256:320]], axis=1),
        jnp.concatenate([row[:, 128:256], row[:, 320:384]], axis=1),
    )


def place(i, k, e):
    return (i * 3 + k) * PER_CHIP + e


def kernel(
    g_hbm, s_hbm, w_hbm, tw_hbm, tf_hbm, tb_hbm, new_ref, ren_ref,
    g, s, w, tw, tf, tb, wall, wsend, what, hsend, hrecv, lsend, lrecv, lf, m,
    out1, in1, x, pb, out2, in2, nsend, nrecv, load, local, send, recv,
):
    me, sl = lax.axis_index("energy"), lax.axis_index("slab")
    chip, core = me // 2, me % 2
    sib = me + 1 - 2 * core
    sign = jnp.where(lax.broadcasted_iota(jnp.int32, (1, 128), 1) < 64, 1.0, -1.0).astype(F32)

    loads = [
        pltpu.make_async_copy(src, dst, load.at[n])
        for n, (src, dst) in enumerate(((s_hbm, s), (g_hbm, g), (w_hbm, w), (tw_hbm, tw), (tf_hbm, tf), (tb_hbm, tb)))
    ]
    for copy in loads:
        copy.start()

    barrier = pltpu.get_barrier_semaphore()
    pl.semaphore_signal(barrier, inc=1, device_id=(me, 1 - sl), device_id_type=MESH)
    pl.semaphore_signal(barrier, inc=1, device_id=(sib, sl), device_id_type=MESH)

    @pl.loop(1, CHIPS)
    def _(n):
        pl.semaphore_signal(barrier, inc=1, device_id=((me + 2 * n) % 128, sl), device_id_type=MESH)

    def remote(src, dst, n, to):
        return pltpu.make_async_remote_copy(
            src_ref=src, dst_ref=dst, send_sem=send.at[n], recv_sem=recv.at[n], device_id=to, device_id_type=MESH
        )

    def spread(src, dst, n):
        @pl.loop(0, CHIPS)
        def _(j):
            dz, dx, dy = (j + 2) % 4, (j + j // 4 + 2) % 4, (j + j // 16 + 2) % 4
            to = ((chip // 16 + dy) % 4) * 16 + ((chip // 4 + dz) % 4) * 4 + (chip + dx) % 4

            @pl.when(to != chip)
            def _():
                remote(src.at[to], dst.at[chip], n, (2 * to + core, sl)).start()

        pltpu.make_async_copy(src.at[chip], dst.at[chip], local.at[n]).start()

    def spread_sent(src, n):
        some = src.at[pl.ds(0, CHIPS - 1)]
        pltpu.make_async_copy(some, some, send.at[n]).wait()

    def spread_here(src, dst, n):
        some = dst.at[pl.ds(0, CHIPS - 1)]
        pltpu.make_async_copy(some, some, recv.at[n]).wait()
        pltpu.make_async_copy(src.at[chip], dst.at[chip], local.at[n]).wait()

    edge = 1 - sl
    loads[0].wait()

    @pl.loop(0, OWN)
    def _(e):
        sr, si = s[e, edge, 0], s[e, edge, 1]
        hsend[e, :, 0:128] = sr[:, :128]
        hsend[e, :, 128:256] = si[:, :128]
        hsend[e, :, 256:320] = sr[:, 128:]
        hsend[e, :, 320:384] = si[:, 128:]

    pl.semaphore_wait(barrier, CHIPS + 1)
    halo = remote(hsend, hrecv, 0, (me, 1 - sl))
    halo.start()

    loads[2].wait()
    mine = wall.at[pl.ds(pl.multiple_of(core * HALF, 32), HALF)]
    mine[:, :E] = w[core, 0].astype(BF16)
    mine[:, E:] = w[core, 1].astype(BF16)
    wsend[:, :E] = w[1 - core, 0].astype(BF16)
    wsend[:, E:] = w[1 - core, 1].astype(BF16)
    swap_w = remote(wsend, mine, 1, (sib, sl))
    swap_w.start()

    loads[1].wait()

    def term(e, slab, j, sr, si):
        gr, gi = g[e, slab, j, 0], g[e, slab, j, 1]
        ir, ii = adjoint_product(sr, si, gr, gi)
        return product(gr, gi, ir, ii)

    def lesser(slab, with_halo):
        holder = slab == core

        @pl.loop(0, OWN)
        def _(e):
            lr, li = term(e, slab, 1, s[e, slab, 0], s[e, slab, 1])
            tr, ti = term(e, slab, 2 - 2 * slab, s[e, 1 - slab, 0], s[e, 1 - slab, 1])
            lr, li = lr + tr, li + ti
            if with_halo:
                tr, ti = term(e, slab, 2 * slab, *unpack(hrecv[e]))
                lr, li = lr + tr, li + ti
            at = OWN * core + e
            lf[at, 0] = lr[:, :128]
            lf[at, 1] = li[:, :128]
            lf[at, 2, :, 0:64] = lr[:, 128:]
            lf[at, 2, :, 64:128] = li[:, 128:]

        @pl.when(jnp.logical_not(holder))
        def _():
            @pl.loop(0, OWN)
            def _(e):
                for k in range(3):
                    lsend[e, :, 128 * k : 128 * k + 128] = lf[OWN * core + e, k].astype(BF16)

            remote(lsend, lrecv, 2, (sib, sl)).start()

        @pl.when(holder)
        def _():
            pltpu.make_async_copy(lrecv, lrecv, recv.at[2]).wait()

            @pl.loop(0, OWN)
            def _(e):
                for k in range(3):
                    lf[OWN * (1 - core) + e, k] = lrecv[e, :, 128 * k : 128 * k + 128].astype(F32)

            for e in range(PER_CHIP):
                for i in range(3):
                    for k in range(3):
                        m[pl.ds(place(i, k, e), CHIPS, stride=PITCH), :] = lf[e, k, pl.ds(i, CHIPS, stride=3), :]

            @pl.loop(0, CHIPS)
            def _(c):
                out1[c] = m[pl.ds(pl.multiple_of(c * PITCH, 8), ROWS), :].astype(BF16)

            spread(out1, in1, 3)

    lesser(sl, False)

    swap_w.wait()
    loads[3].wait()
    for i in range(3):
        full = nt(tw[...], wall[B * i : B * i + B, :]) * SCALE
        what[0, i] = full[:E, :128]
        what[1, i] = full[E:, :128]
        what[2, i, :, 0:64] = full[:E, 128:]
        what[2, i, :, 64:128] = full[:E, 128:]
        what[3, i, :, 0:64] = -full[E:, 128:]
        what[3, i, :, 64:128] = full[E:, 128:]

    halo.wait()
    lesser(edge, True)

    loads[4].wait()
    loads[5].wait()
    spread_here(out1, in1, 3)

    @pl.loop(0, CHIPS)
    def _(c):
        m[pl.ds(pl.multiple_of(c * PITCH, 8), ROWS), :] = in1[c].astype(F32)

    for e in range(PER_CHIP):
        top, low = slice(CHIPS * e, CHIPS * e + CHIPS), slice(E + CHIPS * e, E + CHIPS * e + CHIPS)
        for i in range(3):
            at = 384 * i
            a, b, c = (m[pl.ds(place(i, k, e), CHIPS, stride=PITCH), :] for k in range(3))
            x[top, at : at + 128] = a.astype(BF16)
            x[low, at : at + 128] = b.astype(BF16)
            x[top, at + 128 : at + 256] = b.astype(BF16)
            x[low, at + 128 : at + 256] = (-a).astype(BF16)
            x[top, at + 256 : at + 384] = c.astype(BF16)
            x[low, at + 256 : at + 384] = (pltpu.roll(c, 64, 1) * sign).astype(BF16)

    for i in range(3):
        ghat = nn(tf[...], x[:, 384 * i : 384 * i + 384])
        gr, gi, gm = ghat[:, :128], ghat[:, 128:256], ghat[:, 256:]
        wr, wi = what[0, i], what[1, i]
        pr = gr * wr - gi * wi
        pi = gr * wi + gi * wr
        pm = gm * what[2, i] + pltpu.roll(gm, 64, 1) * what[3, i]
        pb[:E, 0:128] = pr.astype(BF16)
        pb[E:, 0:128] = (-pi).astype(BF16)
        pb[:E, 128:256] = pi.astype(BF16)
        pb[E:, 128:256] = pr.astype(BF16)
        pb[:E, 256:384] = pm.astype(BF16)
        pb[E:, 256:384] = (pltpu.roll(pm, 64, 1) * -sign).astype(BF16)
        fresh = nn(tb[...], pb[...])
        for e in range(PER_CHIP):
            for k in range(3):
                m[pl.ds(place(i, k, e), CHIPS, stride=PITCH), :] = fresh[CHIPS * e : CHIPS * e + CHIPS, 128 * k : 128 * k + 128]

    @pl.loop(0, CHIPS)
    def _(c):
        out2[c] = m[pl.ds(pl.multiple_of(c * PITCH, 8), ROWS), :].astype(BF16)

    spread(out2, in2, 4)
    spread_here(out2, in2, 4)

    @pl.loop(0, CHIPS)
    def _(c):
        m[pl.ds(pl.multiple_of(c * PITCH, 8), ROWS), :] = in2[c].astype(F32)

    for e in range(PER_CHIP):
        for i in range(3):
            for k in range(3):
                lf[e, k, pl.ds(i, CHIPS, stride=3), :] = m[pl.ds(place(i, k, e), CHIPS, stride=PITCH), :]

    @pl.loop(0, OWN)
    def _(e):
        for k in range(3):
            nsend[e, :, 128 * k : 128 * k + 128] = lf[OWN * (1 - core) + e, k].astype(BF16)

    swap_n = remote(nsend, nrecv, 5, (sib, sl))
    swap_n.start()

    def second(e, slab, sr, si):
        new_ref[e, slab, 0] = sr
        new_ref[e, slab, 1] = si
        rr, ri = term(e, slab, 1, sr, si)
        ren_ref[e, slab, 0] = rr.astype(BF16)
        ren_ref[e, slab, 1] = ri.astype(BF16)

    @pl.loop(0, OWN)
    def _(e):
        at = OWN * core + e
        tail = lf[at, 2].astype(BF16)
        second(
            e, core,
            jnp.concatenate([lf[at, 0].astype(BF16), tail[:, :64]], axis=1),
            jnp.concatenate([lf[at, 1].astype(BF16), tail[:, 64:]], axis=1),
        )

    swap_n.wait()

    @pl.loop(0, OWN)
    def _(e):
        second(e, 1 - core, *unpack(nrecv[e]))

    pltpu.make_async_copy(lsend, lsend, send.at[2]).wait()
    spread_sent(out1, 3)
    spread_sent(out2, 4)


def shards(green_ret, sigma_less, screened):
    out = jax.ShapeDtypeStruct(sigma_less.shape, BF16)
    packed = pltpu.VMEM((OWN, B, 2 * B), BF16)
    box = pltpu.VMEM((CHIPS, ROWS, 128), BF16)
    return pl.pallas_call(
        kernel,
        out_shape=(out, out),
        in_specs=[pl.BlockSpec(memory_space=pl.ANY)] * 6,
        out_specs=[pl.BlockSpec(memory_space=pltpu.VMEM)] * 2,
        scratch_shapes=[
            pltpu.VMEM(green_ret.shape, BF16),
            pltpu.VMEM(sigma_less.shape, BF16),
            pltpu.VMEM((2, 2, HALF, E), F32),
            pltpu.VMEM((2 * E, 2 * E), BF16),
            pltpu.VMEM((E, 2 * E), BF16),
            pltpu.VMEM((E, 2 * E), BF16),
            pltpu.VMEM((2 * HALF, 2 * E), BF16),
            pltpu.VMEM((HALF, 2 * E), BF16),
            pltpu.VMEM((4, 3, E, 128), F32),
            packed, packed, packed, packed,
            pltpu.VMEM((PER_CHIP, 3, B, 128), F32),
            pltpu.VMEM((CHIPS * PITCH, 128), F32),
            box, box,
            pltpu.VMEM((2 * E, 1152), BF16),
            pltpu.VMEM((2 * E, 384), BF16),
            box, box, packed, packed,
            pltpu.SemaphoreType.DMA((6,)),
            pltpu.SemaphoreType.DMA((6,)),
            pltpu.SemaphoreType.DMA((6,)),
            pltpu.SemaphoreType.DMA((6,)),
        ],
        compiler_params=pltpu.CompilerParams(collective_id=0, has_side_effects=True, vmem_limit_bytes=50 * 2**20),
        name="wire",
    )(green_ret, sigma_less, jnp.transpose(screened, (1, 2, 3, 0)), *tables())


def solution(mesh):
    in_specs = (
        P("energy", "slab", None, None, None, None),
        P("energy", "slab", None, None, None),
        P(None, "slab", None, "energy"),
    )
    out_specs = (P("energy", "slab", None, None, None), P("energy", "slab", None, None, None))
    return jax.shard_map(shards, mesh=mesh, in_specs=in_specs, out_specs=out_specs, check_vma=False)
```

```python
import functools
import math

import jax
import jax.numpy as jnp
import numpy as np
from jax import lax
from jax.experimental import pallas as pl
from jax.experimental.pallas import tpu as pltpu
from jax.sharding import PartitionSpec as P

MESH = pl.DeviceIdType.MESH
F32, BF16 = jnp.float32, jnp.bfloat16
E, B = 384, 192
CHIPS, PER_CHIP, OWN = 64, 6, 3
ROWS, PITCH = 54, 56
HALF = B * 3 // 2
HALO, LESSER, NEW, SCREEN, THERE, BACK, COPIES = 0, 3, 6, 9, 10, 11, 12
SCALE = 1.0 / (E * math.sqrt(E))


def tables():
    point = np.arange(E)

    def parts(rows, cols):
        angle = (rows[:, None] * cols[None, :] % E) * (2.0 * np.pi / E)
        return np.cos(angle), np.sin(angle)

    def held(core):
        own = [(OWN * core + q) % PER_CHIP for q in range(PER_CHIP)]
        return np.array([PER_CHIP * c + k for k in own for c in range(CHIPS)])

    cos, sin = parts(point, point)
    whole = np.concatenate([np.concatenate([cos, sin], 1), np.concatenate([-sin, cos], 1)], 0)
    there = np.stack([np.concatenate(parts(point, held(core)), 1) for core in range(2)])
    back = np.stack([np.concatenate(parts(held(core), point), 1) for core in range(2)])
    return [t.astype(np.float32).astype(BF16) for t in (whole, there, back)]


def nn(a, b):
    return lax.dot_general(a, b, (((1,), (0,)), ((), ())), preferred_element_type=F32)


def nt(a, b):
    return lax.dot_general(a, b, (((1,), (1,)), ((), ())), preferred_element_type=F32)


def adjoint_product(ar, ai, br, bi):
    return (nt(ar, br) + nt(ai, bi)).astype(BF16), (nt(ai, br) - nt(ar, bi)).astype(BF16)


def product(ar, ai, br, bi):
    return nn(ar, br) - nn(ai, bi), nn(ar, bi) + nn(ai, br)


def unpack(row):
    return (
        jnp.concatenate([row[:, :128], row[:, 256:320]], axis=1),
        jnp.concatenate([row[:, 128:256], row[:, 320:384]], axis=1),
    )


def place(i, k, e):
    return (i * 3 + k) * PER_CHIP + e


def kernel(
    g_hbm, s, w_hbm, tw_hbm, tf_hbm, tb_hbm, new_ref, ren_ref,
    g, w, tw, tf, tb, wall, wsend, what, hsend, hrecv, lsend, lrecv, part, lf, m,
    out1, in1, x, pb, out2, in2, nsend, nrecv, load, local, send, recv, line,
):
    me, sl = lax.axis_index("energy"), lax.axis_index("slab")
    chip, core = me // 2, me % 2
    py, pz, px = chip // 16, (chip // 4) % 4, chip % 4
    sib = me + 1 - 2 * core
    sign = jnp.where(lax.broadcasted_iota(jnp.int32, (1, 128), 1) < 64, 1.0, -1.0).astype(F32)

    def at(dy, dz, dx):
        return ((py + dy) % 4) * 16 + ((pz + dz) % 4) * 4 + (px + dx) % 4

    def signal(sem, device, slab):
        pl.semaphore_signal(sem, inc=1, device_id=(device, slab), device_id_type=MESH)

    barrier = pltpu.get_barrier_semaphore()
    signal(barrier, me, 1 - sl)
    signal(barrier, sib, sl)
    for d in range(1, 4):
        for off in ((0, 0, d), (d, 0, 0), (0, d, 0)):
            signal(barrier, 2 * at(*off) + core, sl)

    loads = [
        pltpu.make_async_copy(src, dst, load.at[n])
        for n, (src, dst) in enumerate(
            ((g_hbm, g), (w_hbm, w), (tw_hbm, tw), (tf_hbm.at[core], tf), (tb_hbm.at[core], tb))
        )
    ]
    for copy in loads:
        copy.start()

    def remote(src, dst, n, to):
        return pltpu.make_async_remote_copy(
            src_ref=src, dst_ref=dst, send_sem=send.at[n], recv_sem=recv.at[n], device_id=to, device_id_type=MESH
        )

    def arrived(dst, n):
        pltpu.make_async_copy(dst, dst, recv.at[n]).wait()

    def sent(src, n):
        pltpu.make_async_copy(src, src, send.at[n]).wait()

    def spread(src, dst, n):
        def message(to):
            src[to] = m[pl.ds(pl.multiple_of(to * PITCH, 8), ROWS), :].astype(BF16)

        for dz in (2, 1, 3, 0):
            @pl.loop(0 if dz else 1, 16)
            def _(j):
                to = at(j // 4, dz, j + j // 4)
                message(to)
                remote(src.at[to], dst.at[chip], n, (2 * to + core, sl)).start()

        message(chip)
        pltpu.make_async_copy(src.at[chip], dst.at[chip], local.at[n]).start()

    def collect(src, dst, n):
        arrived(dst.at[pl.ds(0, CHIPS - 1)], n)
        pltpu.make_async_copy(src.at[chip], dst.at[chip], local.at[n]).wait()

        @pl.loop(0, CHIPS)
        def _(c):
            m[pl.ds(pl.multiple_of(c * PITCH, 8), ROWS), :] = dst[c].astype(F32)

    def pack(dst, re, im):
        dst[:, 0:128] = re[:, :128].astype(BF16)
        dst[:, 128:256] = im[:, :128].astype(BF16)
        dst[:, 256:320] = re[:, 128:].astype(BF16)
        dst[:, 320:384] = im[:, 128:].astype(BF16)

    edge = 1 - sl

    @pl.loop(0, OWN)
    def _(e):
        pack(hsend.at[e], s[e, edge, 0], s[e, edge, 1])

    pl.semaphore_wait(barrier, 11)
    halo = [remote(hsend.at[e], hrecv.at[e], HALO + e, (me, 1 - sl)) for e in range(OWN)]
    for copy in halo:
        copy.start()
    for d in range(1, 4):
        signal(line.at[0], 2 * at(0, 0, d) + core, sl)

    loads[1].wait()
    mine = wall.at[pl.ds(pl.multiple_of(core * HALF, 32), HALF)]
    mine[:, :E] = w[core, 0].astype(BF16)
    mine[:, E:] = w[core, 1].astype(BF16)
    wsend[:, :E] = w[1 - core, 0].astype(BF16)
    wsend[:, E:] = w[1 - core, 1].astype(BF16)
    swap_w = remote(wsend, mine, SCREEN, (sib, sl))
    swap_w.start()
    pl.semaphore_wait(line.at[0], 3)
    for d in range(1, 4):
        signal(line.at[1], 2 * at(d, 0, 0) + core, sl)

    loads[0].wait()

    def term(e, slab, j, sr, si):
        gr, gi = g[e, slab, j, 0], g[e, slab, j, 1]
        ir, ii = adjoint_product(sr, si, gr, gi)
        return product(gr, gi, ir, ii)

    def inside(e, slab):
        lr, li = term(e, slab, 1, s[e, slab, 0], s[e, slab, 1])
        tr, ti = term(e, slab, 2 - 2 * slab, s[e, 1 - slab, 0], s[e, 1 - slab, 1])
        return lr + tr, li + ti

    def deliver(e, slab, lr, li):
        @pl.when(slab == core)
        def _():
            lf[e, 0] = lr[:, :128]
            lf[e, 1] = li[:, :128]
            lf[e, 2, :, 0:64] = lr[:, 128:]
            lf[e, 2, :, 64:128] = li[:, 128:]
            gather(e)

        @pl.when(slab != core)
        def _():
            pack(lsend.at[e], lr, li)
            remote(lsend.at[e], lrecv.at[e], LESSER + e, (sib, sl)).start()

    def gather(q):
        for i in range(3):
            for k in range(3):
                m[pl.ds(place(i, k, q), CHIPS, stride=PITCH), :] = lf[q, k, pl.ds(i, CHIPS, stride=3), :]

    def receive(e):
        arrived(lrecv.at[e], LESSER + e)
        for k in range(3):
            lf[OWN + e, k] = lrecv[e, :, 128 * k : 128 * k + 128].astype(F32)
        gather(OWN + e)

    for e in range(OWN):
        deliver(e, sl, *inside(e, sl))

    @pl.loop(0, OWN)
    def _(e):
        part[e, 0], part[e, 1] = inside(e, edge)

    pl.semaphore_wait(line.at[1], 3)

    swap_w.wait()
    loads[2].wait()
    for i in range(3):
        full = nt(tw[...], wall[B * i : B * i + B, :]) * SCALE
        what[0, i] = full[:E, :128]
        what[1, i] = full[E:, :128]
        what[2, i, :, 0:64] = full[:E, 128:]
        what[2, i, :, 64:128] = full[:E, 128:]
        what[3, i, :, 0:64] = -full[E:, 128:]
        what[3, i, :, 64:128] = full[E:, 128:]

    @pl.when(core == sl)
    def _():
        for e in range(OWN):
            receive(e)

    for e in range(OWN):
        halo[e].wait()
        tr, ti = term(e, edge, 2 * edge, *unpack(hrecv[e]))
        deliver(e, edge, part[e, 0] + tr, part[e, 1] + ti)

        if e == 1:
            @pl.when(core == sl)
            def _():
                spread(out1, in1, THERE)

    @pl.when(core == edge)
    def _():
        for e in range(OWN):
            receive(e)
        spread(out1, in1, THERE)

    loads[3].wait()
    loads[4].wait()
    collect(out1, in1, THERE)

    for q in range(PER_CHIP):
        top, low = slice(CHIPS * q, CHIPS * q + CHIPS), slice(E + CHIPS * q, E + CHIPS * q + CHIPS)
        for i in range(3):
            a, b, c = (m[pl.ds(place(i, k, q), CHIPS, stride=PITCH), :] for k in range(3))
            x[top, 384 * i : 384 * i + 128] = a.astype(BF16)
            x[low, 384 * i : 384 * i + 128] = b.astype(BF16)
            x[top, 384 * i + 128 : 384 * i + 256] = b.astype(BF16)
            x[low, 384 * i + 128 : 384 * i + 256] = (-a).astype(BF16)
            x[top, 384 * i + 256 : 384 * i + 384] = c.astype(BF16)
            x[low, 384 * i + 256 : 384 * i + 384] = (pltpu.roll(c, 64, 1) * sign).astype(BF16)

    for i in range(3):
        ghat = nn(tf[...], x[:, 384 * i : 384 * i + 384])
        gr, gi, gm = ghat[:, :128], ghat[:, 128:256], ghat[:, 256:]
        wr, wi = what[0, i], what[1, i]
        pr = gr * wr - gi * wi
        pi = gr * wi + gi * wr
        pm = gm * what[2, i] + pltpu.roll(gm, 64, 1) * what[3, i]
        pb[:E, 0:128] = pr.astype(BF16)
        pb[E:, 0:128] = (-pi).astype(BF16)
        pb[:E, 128:256] = pi.astype(BF16)
        pb[E:, 128:256] = pr.astype(BF16)
        pb[:E, 256:384] = pm.astype(BF16)
        pb[E:, 256:384] = (pltpu.roll(pm, 64, 1) * -sign).astype(BF16)
        fresh = nn(tb[...], pb[...])
        for q in range(PER_CHIP):
            for k in range(3):
                m[pl.ds(place(i, k, q), CHIPS, stride=PITCH), :] = fresh[CHIPS * q : CHIPS * q + CHIPS, 128 * k : 128 * k + 128]

    spread(out2, in2, BACK)
    collect(out2, in2, BACK)

    def restore(q):
        for i in range(3):
            for k in range(3):
                lf[q, k, pl.ds(i, CHIPS, stride=3), :] = m[pl.ds(place(i, k, q), CHIPS, stride=PITCH), :]

    def second(e, slab, sr, si):
        new_ref[e, slab, 0] = sr
        new_ref[e, slab, 1] = si
        rr, ri = term(e, slab, 1, sr, si)
        ren_ref[e, slab, 0] = rr.astype(BF16)
        ren_ref[e, slab, 1] = ri.astype(BF16)

    swap_n = [remote(nsend.at[e], nrecv.at[e], NEW + e, (sib, sl)) for e in range(OWN)]
    for e in range(OWN):
        restore(OWN + e)
        for k in range(3):
            nsend[e, :, 128 * k : 128 * k + 128] = lf[OWN + e, k].astype(BF16)
        swap_n[e].start()

    for e in range(OWN):
        restore(e)
        tail = lf[e, 2].astype(BF16)
        second(
            e, core,
            jnp.concatenate([lf[e, 0].astype(BF16), tail[:, :64]], axis=1),
            jnp.concatenate([lf[e, 1].astype(BF16), tail[:, 64:]], axis=1),
        )

    for e in range(OWN):
        swap_n[e].wait()
        second(e, 1 - core, *unpack(nrecv[e]))

    for e in range(OWN):
        sent(lsend.at[e], LESSER + e)
    sent(out1.at[pl.ds(0, CHIPS - 1)], THERE)
    sent(out2.at[pl.ds(0, CHIPS - 1)], BACK)


def shards(green_ret, sigma_less, screened):
    out = jax.ShapeDtypeStruct(sigma_less.shape, BF16)
    packed = pltpu.VMEM((OWN, B, 2 * B), BF16)
    box = pltpu.VMEM((CHIPS, ROWS, 128), BF16)
    return pl.pallas_call(
        kernel,
        out_shape=(out, out),
        in_specs=[pl.BlockSpec(memory_space=pltpu.VMEM if n == 1 else pltpu.HBM) for n in range(6)],
        out_specs=[pl.BlockSpec(memory_space=pltpu.VMEM)] * 2,
        scratch_shapes=[
            pltpu.VMEM(green_ret.shape, BF16),
            pltpu.VMEM((2, 2, HALF, E), F32),
            pltpu.VMEM((2 * E, 2 * E), BF16),
            pltpu.VMEM((E, 2 * E), BF16),
            pltpu.VMEM((E, 2 * E), BF16),
            pltpu.VMEM((2 * HALF, 2 * E), BF16),
            pltpu.VMEM((HALF, 2 * E), BF16),
            pltpu.VMEM((4, 3, E, 128), F32),
            packed, packed, packed, packed,
            pltpu.VMEM((OWN, 2, B, B), F32),
            pltpu.VMEM((PER_CHIP, 3, B, 128), F32),
            pltpu.VMEM((CHIPS * PITCH, 128), F32),
            box, box,
            pltpu.VMEM((2 * E, 1152), BF16),
            pltpu.VMEM((2 * E, 384), BF16),
            box, box, packed, packed,
            pltpu.SemaphoreType.DMA((5,)),
            pltpu.SemaphoreType.DMA((COPIES,)),
            pltpu.SemaphoreType.DMA((COPIES,)),
            pltpu.SemaphoreType.DMA((COPIES,)),
            pltpu.SemaphoreType.REGULAR((2,)),
        ],
        compiler_params=pltpu.CompilerParams(collective_id=0, has_side_effects=True, vmem_limit_bytes=50 * 2**20),
        name="wire",
    )(green_ret, sigma_less, jnp.transpose(screened, (1, 2, 3, 0)), *tables())


def solution(mesh):
    in_specs = (
        P("energy", "slab", None, None, None, None),
        P("energy", "slab", None, None, None),
        P(None, "slab", None, "energy"),
    )
    out_specs = (P("energy", "slab", None, None, None), P("energy", "slab", None, None, None))
    return jax.shard_map(shards, mesh=mesh, in_specs=in_specs, out_specs=out_specs, check_vma=False)
```

```python
import functools
import math

import jax
import jax.numpy as jnp
import numpy as np
from jax import lax
from jax.experimental import pallas as pl
from jax.experimental.pallas import tpu as pltpu
from jax.sharding import PartitionSpec as P

MESH = pl.DeviceIdType.MESH
F32, BF16 = jnp.float32, jnp.bfloat16
E, B = 384, 192
CHIPS, PER_CHIP, OWN = 64, 6, 3
PITCH = 32
SETS = (((0, 0), (0, 1), (0, 2), (1, 2)), ((1, 0), (1, 1), (2, 0), (2, 1), (2, 2)))
HALF = B * 3 // 2
HALO, LESSER, NEW, SCREEN, THERE, BACK, COPIES = 0, 3, 9, 15, 17, 19, 21
EARLY = 1
SCALE = 1.0 / (E * math.sqrt(E))


def tables():
    point = np.arange(E)

    def parts(rows, cols):
        angle = (rows[:, None] * cols[None, :] % E) * (2.0 * np.pi / E)
        return np.cos(angle), np.sin(angle)

    def held(core):
        own = [(OWN * core + q) % PER_CHIP for q in range(PER_CHIP)]
        return np.array([PER_CHIP * c + k for k in own for c in range(CHIPS)])

    cos, sin = parts(point, point)
    whole = np.concatenate([np.concatenate([cos, sin], 1), np.concatenate([-sin, cos], 1)], 0)
    there = np.stack([np.concatenate(parts(point, held(core)), 1) for core in range(2)])
    back = np.stack([np.concatenate(parts(held(core), point), 1) for core in range(2)])
    return [t.astype(np.float32).astype(BF16) for t in (whole, there, back)]


def nn(a, b):
    return lax.dot_general(a, b, (((1,), (0,)), ((), ())), preferred_element_type=F32)


def nt(a, b):
    return lax.dot_general(a, b, (((1,), (1,)), ((), ())), preferred_element_type=F32)


def adjoint_product(ar, ai, br, bi):
    return (nt(ar, br) + nt(ai, bi)).astype(BF16), (nt(ai, br) - nt(ar, bi)).astype(BF16)


def product(ar, ai, br, bi):
    return nn(ar, br) - nn(ai, bi), nn(ar, bi) + nn(ai, br)


def unpack(row):
    return (
        jnp.concatenate([row[:, :128], row[:, 256:320]], axis=1),
        jnp.concatenate([row[:, 128:256], row[:, 320:384]], axis=1),
    )


def comb(t, q):
    return pl.ds(t * PER_CHIP + q, CHIPS, stride=PITCH)


def kernel(
    g_hbm, s, w_hbm, tw_hbm, tf_hbm, tb_hbm, new_ref, ren_ref,
    g, w, tw, tf, tb, wall, what, hsend, hrecv, part, lf, x, pb,
    m0, m1, ls0, ls1, lr0, lr1, out0, out1, in0, in1, bout0, bout1, bin0, bin1, ns0, ns1, nr0, nr1,
    load, local, send, recv, line,
):
    me, sl = lax.axis_index("energy"), lax.axis_index("slab")
    chip, core = me // 2, me % 2
    py, pz, px = chip // 16, (chip // 4) % 4, chip % 4
    sib = me + 1 - 2 * core
    m, ls, lr, out, inn = (m0, m1), (ls0, ls1), (lr0, lr1), (out0, out1), (in0, in1)
    bout, bin, ns, nr = (bout0, bout1), (bin0, bin1), (ns0, ns1), (nr0, nr1)
    sign = jnp.where(lax.broadcasted_iota(jnp.int32, (1, 128), 1) < 64, 1.0, -1.0).astype(F32)

    def at(dy, dz, dx):
        return ((py + dy) % 4) * 16 + ((pz + dz) % 4) * 4 + (px + dx) % 4

    def signal(sem, device, slab):
        pl.semaphore_signal(sem, inc=1, device_id=(device, slab), device_id_type=MESH)

    barrier = pltpu.get_barrier_semaphore()
    signal(barrier, me, 1 - sl)
    signal(barrier, sib, sl)
    for d in range(1, 4):
        for off in ((0, 0, d), (d, 0, 0), (0, d, 0)):
            signal(barrier, 2 * at(*off) + core, sl)

    loads = [
        pltpu.make_async_copy(src, dst, load.at[n])
        for n, (src, dst) in enumerate(
            ((g_hbm, g), (w_hbm, w), (tw_hbm, tw), (tf_hbm.at[core], tf), (tb_hbm.at[core], tb))
        )
    ]
    for copy in loads:
        copy.start()

    def remote(src, dst, n, to):
        return pltpu.make_async_remote_copy(
            src_ref=src, dst_ref=dst, send_sem=send.at[n], recv_sem=recv.at[n], device_id=to, device_id_type=MESH
        )

    def arrived(dst, n):
        pltpu.make_async_copy(dst, dst, recv.at[n]).wait()

    def sent(src, n):
        pltpu.make_async_copy(src, src, send.at[n]).wait()

    def each(stage, do):
        for c in range(2):
            @pl.when(core == c)
            def _():
                do(c ^ stage)

    def spread(t, src, dst, n):
        rows = src.shape[1]

        def message(to):
            src[to] = m[t][pl.ds(pl.multiple_of(to * PITCH, 8), rows), :].astype(BF16)

        for dz in (2, 1, 3, 0):
            @pl.loop(0 if dz else 1, 16)
            def _(j):
                to = at(j // 4, dz, j + j // 4)
                message(to)
                remote(src.at[to], dst.at[chip], n, (2 * to + core, sl)).start()

        message(chip)
        pltpu.make_async_copy(src.at[chip], dst.at[chip], local.at[n]).start()

    def collect(t, src, dst, n):
        arrived(dst.at[pl.ds(0, CHIPS - 1)], n)
        pltpu.make_async_copy(src.at[chip], dst.at[chip], local.at[n]).wait()

        @pl.loop(0, CHIPS)
        def _(c):
            m[t][pl.ds(pl.multiple_of(c * PITCH, 8), dst.shape[1]), :] = dst[c].astype(F32)

    def pack(dst, re, im):
        dst[:, 0:128] = re[:, :128].astype(BF16)
        dst[:, 128:256] = im[:, :128].astype(BF16)
        dst[:, 256:320] = re[:, 128:].astype(BF16)
        dst[:, 320:384] = im[:, 128:].astype(BF16)

    edge = 1 - sl

    @pl.loop(0, OWN)
    def _(e):
        pack(hsend.at[e], s[e, edge, 0], s[e, edge, 1])

    pl.semaphore_wait(barrier, 11)
    halo = [remote(hsend.at[e], hrecv.at[e], HALO + e, (me, 1 - sl)) for e in range(OWN)]
    for copy in halo:
        copy.start()
    for d in range(1, 4):
        signal(line.at[0], 2 * at(0, 0, d) + core, sl)

    loads[1].wait()
    swap_w = []
    for slab in range(2):
        mine = wall.at[slab, pl.ds(pl.multiple_of(core * HALF, 32), HALF)]
        mine[:, :E] = w[slab, 0].astype(BF16)
        mine[:, E:] = w[slab, 1].astype(BF16)
        swap_w.append(remote(mine, mine, SCREEN + slab, (sib, sl)))
        swap_w[slab].start()
    pl.semaphore_wait(line.at[0], 3)
    for d in range(1, 4):
        signal(line.at[1], 2 * at(d, 0, 0) + core, sl)

    loads[0].wait()

    def term(e, slab, j, sr, si):
        gr, gi = g[e, slab, j, 0], g[e, slab, j, 1]
        ir, ii = adjoint_product(sr, si, gr, gi)
        return product(gr, gi, ir, ii)

    def inside(e, slab):
        lr, li = term(e, slab, 1, s[e, slab, 0], s[e, slab, 1])
        tr, ti = term(e, slab, 2 - 2 * slab, s[e, 1 - slab, 0], s[e, 1 - slab, 1])
        return lr + tr, li + ti

    def scatter(e, re, im):
        lf[e, 0] = re[:, :128]
        lf[e, 1] = im[:, :128]
        lf[e, 2, :, 0:64] = re[:, 128:]
        lf[e, 2, :, 64:128] = im[:, 128:]

    def deliver(stage, e):
        def do(mine):
            for t, (i, k) in enumerate(SETS[mine]):
                m[mine][comb(t, e), :] = lf[e, k, pl.ds(i, CHIPS, stride=3), :]
            other = 1 - mine
            for t, (i, k) in enumerate(SETS[other]):
                ls[other][e, t] = lf[e, k, pl.ds(i, CHIPS, stride=3), :].astype(BF16)
            remote(ls[other].at[e], lr[other].at[e], LESSER + OWN * other + e, (sib, sl)).start()

        each(stage, do)

    def receive(mine):
        for e in range(OWN):
            arrived(lr[mine].at[e], LESSER + OWN * mine + e)
            for t in range(len(SETS[mine])):
                m[mine][comb(t, OWN + e), :] = lr[mine][e, t].astype(F32)

    def send_there(mine):
        spread(mine, out[mine], inn[mine], THERE + mine)

    for e in range(OWN):
        scatter(e, *inside(e, sl))
        deliver(0, e)

    @pl.loop(0, OWN)
    def _(e):
        part[e, 0], part[e, 1] = inside(e, edge)

    pl.semaphore_wait(line.at[1], 3)

    for copy in swap_w:
        copy.wait()
    loads[2].wait()
    slab_of = ((sl + core) % 2, (sl + core + 1) % 2)

    def pairs(i, full):
        what[0, i] = full[:E, :128]
        what[1, i] = full[E:, :128]

    def tail(i, full):
        what[2, i, :, 0:64] = full[:E]
        what[2, i, :, 64:128] = full[:E]
        what[3, i, :, 0:64] = -full[E:]
        what[3, i, :, 64:128] = full[E:]

    def transform(c, lo, hi):
        return nt(tw[...], wall[slab_of[c], lo:hi, :]) * SCALE

    for c, i in ((0, 0), (1, 2)):
        full = transform(c, B * i, B * i + B)
        pairs(i, full)
        tail(i, full[:, 128:])
    pairs(1, transform(1, B, B + 128))
    tail(1, transform(0, B + 128, 2 * B))

    each(0, receive)
    for e in range(OWN):
        halo[e].wait()
        tr, ti = term(e, edge, 2 * edge, *unpack(hrecv[e]))
        scatter(e, part[e, 0] + tr, part[e, 1] + ti)
        deliver(1, e)
        if e == EARLY:
            each(0, send_there)

    each(1, receive)
    each(1, send_there)

    loads[3].wait()
    loads[4].wait()

    def convolve(mine):
        collect(mine, out[mine], inn[mine], THERE + mine)
        tiles = SETS[mine]
        wide = 128 * len(tiles)
        lanes = [slice(128 * t, 128 * t + 128) for t in range(len(tiles))]
        for q in range(PER_CHIP):
            top, low = slice(CHIPS * q, CHIPS * q + CHIPS), slice(E + CHIPS * q, E + CHIPS * q + CHIPS)
            for t, (i, k) in enumerate(tiles):
                a = m[mine][comb(t, q), :]
                x[top, lanes[t]] = a.astype(BF16)
                if k == 0:
                    x[low, lanes[t + 1]] = (-a).astype(BF16)
                elif k == 1:
                    x[low, lanes[t - 1]] = a.astype(BF16)
                else:
                    x[low, lanes[t]] = (pltpu.roll(a, 64, 1) * sign).astype(BF16)

        ghat = nn(tf[...], x[:, :wide])
        for t, (i, k) in enumerate(tiles):
            if k == 0:
                gr, gi = ghat[:, lanes[t]], ghat[:, lanes[t + 1]]
                wr, wi = what[0, i], what[1, i]
                pr = gr * wr - gi * wi
                pi = gr * wi + gi * wr
                pb[:E, lanes[t]] = pr.astype(BF16)
                pb[E:, lanes[t]] = (-pi).astype(BF16)
                pb[:E, lanes[t + 1]] = pi.astype(BF16)
                pb[E:, lanes[t + 1]] = pr.astype(BF16)
            elif k == 2:
                gm = ghat[:, lanes[t]]
                pm = gm * what[2, i] + pltpu.roll(gm, 64, 1) * what[3, i]
                pb[:E, lanes[t]] = pm.astype(BF16)
                pb[E:, lanes[t]] = (pltpu.roll(pm, 64, 1) * -sign).astype(BF16)
        fresh = nn(tb[...], pb[:, :wide])
        for q in range(PER_CHIP):
            for t in range(len(tiles)):
                m[mine][comb(t, q), :] = fresh[CHIPS * q : CHIPS * q + CHIPS, lanes[t]]
        spread(mine, bout[mine], bin[mine], BACK + mine)

    each(0, convolve)
    each(1, convolve)

    def second(e, slab):
        last = lf[e, 2].astype(BF16)
        sr = jnp.concatenate([lf[e, 0].astype(BF16), last[:, :64]], axis=1)
        si = jnp.concatenate([lf[e, 1].astype(BF16), last[:, 64:]], axis=1)
        new_ref[e, slab, 0] = sr
        new_ref[e, slab, 1] = si
        rr, ri = term(e, slab, 1, sr, si)
        ren_ref[e, slab, 0] = rr.astype(BF16)
        ren_ref[e, slab, 1] = ri.astype(BF16)

    for stage, slab in ((0, sl), (1, edge)):
        def give(mine):
            collect(mine, bout[mine], bin[mine], BACK + mine)
            for e in range(OWN):
                for t in range(len(SETS[mine])):
                    ns[mine][e, t] = m[mine][comb(t, OWN + e), :].astype(BF16)
                remote(ns[mine].at[e], nr[mine].at[e], NEW + OWN * mine + e, (sib, sl)).start()
            for e in range(OWN):
                for t, (i, k) in enumerate(SETS[mine]):
                    lf[e, k, pl.ds(i, CHIPS, stride=3), :] = m[mine][comb(t, e), :]

        def take(mine):
            other = 1 - mine
            for e in range(OWN):
                arrived(nr[other].at[e], NEW + OWN * other + e)
                for t, (i, k) in enumerate(SETS[other]):
                    lf[e, k, pl.ds(i, CHIPS, stride=3), :] = nr[other][e, t].astype(F32)

        each(stage, give)
        each(stage, take)
        for e in range(OWN):
            second(e, slab)

    for t in range(2):
        for e in range(OWN):
            sent(ls[t].at[e], LESSER + OWN * t + e)
            sent(ns[t].at[e], NEW + OWN * t + e)
        sent(out[t].at[pl.ds(0, CHIPS - 1)], THERE + t)
        sent(bout[t].at[pl.ds(0, CHIPS - 1)], BACK + t)


def shards(green_ret, sigma_less, screened):
    out = jax.ShapeDtypeStruct(sigma_less.shape, BF16)
    packed = pltpu.VMEM((OWN, B, 2 * B), BF16)

    def both(make):
        return [make(len(tiles)) for tiles in SETS]

    def tiles(n):
        return pltpu.VMEM((OWN, n, CHIPS, 128), BF16)

    def box(n):
        return pltpu.VMEM((CHIPS, n * PER_CHIP, 128), BF16)

    return pl.pallas_call(
        kernel,
        out_shape=(out, out),
        in_specs=[pl.BlockSpec(memory_space=pltpu.VMEM if n == 1 else pltpu.HBM) for n in range(6)],
        out_specs=[pl.BlockSpec(memory_space=pltpu.VMEM)] * 2,
        scratch_shapes=[
            pltpu.VMEM(green_ret.shape, BF16),
            pltpu.VMEM((2, 2, HALF, E), F32),
            pltpu.VMEM((2 * E, 2 * E), BF16),
            pltpu.VMEM((E, 2 * E), BF16),
            pltpu.VMEM((E, 2 * E), BF16),
            pltpu.VMEM((2, 2 * HALF, 2 * E), BF16),
            pltpu.VMEM((4, 3, E, 128), F32),
            packed, packed,
            pltpu.VMEM((OWN, 2, B, B), F32),
            pltpu.VMEM((OWN, 3, B, 128), F32),
            pltpu.VMEM((2 * E, 640), BF16),
            pltpu.VMEM((2 * E, 640), BF16),
            *[pltpu.VMEM((CHIPS * PITCH, 128), F32)] * 2,
            *both(tiles), *both(tiles), *both(box), *both(box), *both(box), *both(box), *both(tiles), *both(tiles),
            pltpu.SemaphoreType.DMA((5,)),
            pltpu.SemaphoreType.DMA((COPIES,)),
            pltpu.SemaphoreType.DMA((COPIES,)),
            pltpu.SemaphoreType.DMA((COPIES,)),
            pltpu.SemaphoreType.REGULAR((2,)),
        ],
        compiler_params=pltpu.CompilerParams(collective_id=0, has_side_effects=True, vmem_limit_bytes=50 * 2**20),
        name="wire",
    )(green_ret, sigma_less, jnp.transpose(screened, (1, 2, 3, 0)), *tables())


def solution(mesh):
    in_specs = (
        P("energy", "slab", None, None, None, None),
        P("energy", "slab", None, None, None),
        P(None, "slab", None, "energy"),
    )
    out_specs = (P("energy", "slab", None, None, None), P("energy", "slab", None, None, None))
    return jax.shard_map(shards, mesh=mesh, in_specs=in_specs, out_specs=out_specs, check_vma=False)
```

```python
import functools
import math

import jax
import jax.numpy as jnp
import numpy as np
from jax import lax
from jax.experimental import pallas as pl
from jax.experimental.pallas import tpu as pltpu
from jax.sharding import PartitionSpec as P

MESH = pl.DeviceIdType.MESH
F32, BF16 = jnp.float32, jnp.bfloat16
E, B = 384, 192
CHIPS, PER_CHIP, OWN = 64, 6, 3
PITCH = 32
SETS = (((0, 0), (0, 1), (0, 2), (1, 2)), ((1, 0), (1, 1), (2, 0), (2, 1), (2, 2)))
HALF = B * 3 // 2
HALO, LESSER, NEW, SCREEN, THERE, BACK, COPIES = 0, 3, 9, 15, 17, 19, 21
EARLY = 1
SCALE = 1.0 / (E * math.sqrt(E))


def tables():
    point = np.arange(E)

    def parts(rows, cols):
        angle = (rows[:, None] * cols[None, :] % E) * (2.0 * np.pi / E)
        return np.cos(angle), np.sin(angle)

    def held(core):
        own = [(OWN * core + q) % PER_CHIP for q in range(PER_CHIP)]
        return np.array([PER_CHIP * c + k for k in own for c in range(CHIPS)])

    cos, sin = parts(point, point)
    whole = np.concatenate([np.concatenate([cos, sin], 1), np.concatenate([-sin, cos], 1)], 0)
    there = np.stack([np.concatenate(parts(point, held(core)), 1) for core in range(2)])
    back = np.stack([np.concatenate(parts(held(core), point), 1) for core in range(2)])
    return [t.astype(np.float32).astype(BF16) for t in (whole, there, back)]


def nn(a, b):
    return lax.dot_general(a, b, (((1,), (0,)), ((), ())), preferred_element_type=F32)


def nt(a, b):
    return lax.dot_general(a, b, (((1,), (1,)), ((), ())), preferred_element_type=F32)


def adjoint_product(ar, ai, br, bi):
    return (nt(ar, br) + nt(ai, bi)).astype(BF16), (nt(ai, br) - nt(ar, bi)).astype(BF16)


def product(ar, ai, br, bi):
    return nn(ar, br) - nn(ai, bi), nn(ar, bi) + nn(ai, br)


def unpack(row):
    return (
        jnp.concatenate([row[:, :128], row[:, 256:320]], axis=1),
        jnp.concatenate([row[:, 128:256], row[:, 320:384]], axis=1),
    )


def comb(t, q):
    return pl.ds(t * PER_CHIP + q, CHIPS, stride=PITCH)


def kernel(
    g_hbm, s, w_hbm, tw_hbm, tf_hbm, tb_hbm, new_ref, ren_ref,
    g, w, tw, tf, tb, wall, what, hsend, hrecv, part, lf, x, pb,
    m0, m1, ls0, ls1, lr0, lr1, out0, out1, in0, in1, bout0, bout1, bin0, bin1, ns0, ns1, nr0, nr1,
    load, local, send, recv, line,
):
    me, sl = lax.axis_index("energy"), lax.axis_index("slab")
    chip, core = me // 2, me % 2
    py, pz, px = chip // 16, (chip // 4) % 4, chip % 4
    sib = me + 1 - 2 * core
    m, ls, lr, out, inn = (m0, m1), (ls0, ls1), (lr0, lr1), (out0, out1), (in0, in1)
    bout, bin, ns, nr = (bout0, bout1), (bin0, bin1), (ns0, ns1), (nr0, nr1)
    sign = jnp.where(lax.broadcasted_iota(jnp.int32, (1, 128), 1) < 64, 1.0, -1.0).astype(F32)

    def at(dy, dz, dx):
        return ((py + dy) % 4) * 16 + ((pz + dz) % 4) * 4 + (px + dx) % 4

    def signal(sem, device, slab):
        pl.semaphore_signal(sem, inc=1, device_id=(device, slab), device_id_type=MESH)

    barrier = pltpu.get_barrier_semaphore()
    signal(barrier, me, 1 - sl)
    signal(barrier, sib, sl)
    for d in range(1, 4):
        for off in ((0, 0, d), (d, 0, 0), (0, d, 0)):
            signal(barrier, 2 * at(*off) + core, sl)

    loads = [
        pltpu.make_async_copy(src, dst, load.at[n])
        for n, (src, dst) in enumerate(
            ((g_hbm, g), (w_hbm, w), (tw_hbm, tw), (tf_hbm.at[core], tf), (tb_hbm.at[core], tb))
        )
    ]
    for copy in loads:
        copy.start()

    def remote(src, dst, n, to):
        return pltpu.make_async_remote_copy(
            src_ref=src, dst_ref=dst, send_sem=send.at[n], recv_sem=recv.at[n], device_id=to, device_id_type=MESH
        )

    def arrived(dst, n):
        pltpu.make_async_copy(dst, dst, recv.at[n]).wait()

    def sent(src, n):
        pltpu.make_async_copy(src, src, send.at[n]).wait()

    def each(stage, do):
        for c in range(2):
            @pl.when(core == c)
            def _():
                do(c ^ stage)

    def spread(t, src, dst, n):
        rows = src.shape[1]

        def message(to):
            src[to] = m[t][pl.ds(pl.multiple_of(to * PITCH, 8), rows), :].astype(BF16)

        for dz in (2, 1, 3, 0):
            @pl.loop(0 if dz else 1, 16)
            def _(j):
                to = at(j // 4, dz, j + j // 4)
                message(to)
                remote(src.at[to], dst.at[chip], n, (2 * to + core, sl)).start()

        message(chip)
        pltpu.make_async_copy(src.at[chip], dst.at[chip], local.at[n]).start()

    def collect(t, src, dst, n):
        arrived(dst.at[pl.ds(0, CHIPS - 1)], n)
        pltpu.make_async_copy(src.at[chip], dst.at[chip], local.at[n]).wait()

        @pl.loop(0, CHIPS)
        def _(c):
            m[t][pl.ds(pl.multiple_of(c * PITCH, 8), dst.shape[1]), :] = dst[c].astype(F32)

    def pack(dst, re, im):
        dst[:, 0:128] = re[:, :128].astype(BF16)
        dst[:, 128:256] = im[:, :128].astype(BF16)
        dst[:, 256:320] = re[:, 128:].astype(BF16)
        dst[:, 320:384] = im[:, 128:].astype(BF16)

    edge = 1 - sl

    @pl.loop(0, OWN)
    def _(e):
        pack(hsend.at[e], s[e, edge, 0], s[e, edge, 1])

    pl.semaphore_wait(barrier, 11)
    for e in range(OWN):
        for row in range(0, B, 32):
            piece = (e, pl.ds(row, 32))
            remote(hsend.at[piece], hrecv.at[piece], HALO + e, (me, 1 - sl)).start()
    for d in range(1, 4):
        signal(line.at[0], 2 * at(0, 0, d) + core, sl)

    loads[1].wait()
    swap_w = []
    for slab in range(2):
        mine = wall.at[slab, pl.ds(pl.multiple_of(core * HALF, 32), HALF)]
        mine[:, :E] = w[slab, 0].astype(BF16)
        mine[:, E:] = w[slab, 1].astype(BF16)
        swap_w.append(remote(mine, mine, SCREEN + slab, (sib, sl)))
        swap_w[slab].start()
    pl.semaphore_wait(line.at[0], 3)
    for d in range(1, 4):
        signal(line.at[1], 2 * at(d, 0, 0) + core, sl)

    loads[0].wait()

    def term(e, slab, j, sr, si):
        gr, gi = g[e, slab, j, 0], g[e, slab, j, 1]
        ir, ii = adjoint_product(sr, si, gr, gi)
        return product(gr, gi, ir, ii)

    def inside(e, slab):
        lr, li = term(e, slab, 1, s[e, slab, 0], s[e, slab, 1])
        tr, ti = term(e, slab, 2 - 2 * slab, s[e, 1 - slab, 0], s[e, 1 - slab, 1])
        return lr + tr, li + ti

    def scatter(e, re, im):
        lf[e, 0] = re[:, :128]
        lf[e, 1] = im[:, :128]
        lf[e, 2, :, 0:64] = re[:, 128:]
        lf[e, 2, :, 64:128] = im[:, 128:]

    def deliver(stage, e):
        def do(mine):
            for t, (i, k) in enumerate(SETS[mine]):
                m[mine][comb(t, e), :] = lf[e, k, pl.ds(i, CHIPS, stride=3), :]
            other = 1 - mine
            for t, (i, k) in enumerate(SETS[other]):
                ls[other][e, t] = lf[e, k, pl.ds(i, CHIPS, stride=3), :].astype(BF16)
            remote(ls[other].at[e], lr[other].at[e], LESSER + OWN * other + e, (sib, sl)).start()

        each(stage, do)

    def receive(mine):
        for e in range(OWN):
            arrived(lr[mine].at[e], LESSER + OWN * mine + e)
            for t in range(len(SETS[mine])):
                m[mine][comb(t, OWN + e), :] = lr[mine][e, t].astype(F32)

    def send_there(mine):
        spread(mine, out[mine], inn[mine], THERE + mine)

    for e in range(OWN):
        scatter(e, *inside(e, sl))
        deliver(0, e)

    @pl.loop(0, OWN)
    def _(e):
        part[e, 0], part[e, 1] = inside(e, edge)

    pl.semaphore_wait(line.at[1], 3)

    for copy in swap_w:
        copy.wait()
    loads[2].wait()
    slab_of = ((sl + core) % 2, (sl + core + 1) % 2)

    def pairs(i, full):
        what[0, i] = full[:E, :128]
        what[1, i] = full[E:, :128]

    def tail(i, full):
        what[2, i, :, 0:64] = full[:E]
        what[2, i, :, 64:128] = full[:E]
        what[3, i, :, 0:64] = -full[E:]
        what[3, i, :, 64:128] = full[E:]

    def transform(c, lo, hi):
        return nt(tw[...], wall[slab_of[c], lo:hi, :]) * SCALE

    for c, i in ((0, 0), (1, 2)):
        full = transform(c, B * i, B * i + B)
        pairs(i, full)
        tail(i, full[:, 128:])
    pairs(1, transform(1, B, B + 128))
    tail(1, transform(0, B + 128, 2 * B))

    each(0, receive)
    for e in range(OWN):
        arrived(hrecv.at[e], HALO + e)
        tr, ti = term(e, edge, 2 * edge, *unpack(hrecv[e]))
        scatter(e, part[e, 0] + tr, part[e, 1] + ti)
        deliver(1, e)
        if e == EARLY:
            each(0, send_there)

    each(1, receive)
    each(1, send_there)

    loads[3].wait()
    loads[4].wait()

    def convolve(mine):
        collect(mine, out[mine], inn[mine], THERE + mine)
        tiles = SETS[mine]
        wide = 128 * len(tiles)
        lanes = [slice(128 * t, 128 * t + 128) for t in range(len(tiles))]
        for q in range(PER_CHIP):
            top, low = slice(CHIPS * q, CHIPS * q + CHIPS), slice(E + CHIPS * q, E + CHIPS * q + CHIPS)
            for t, (i, k) in enumerate(tiles):
                a = m[mine][comb(t, q), :]
                x[top, lanes[t]] = a.astype(BF16)
                if k == 0:
                    x[low, lanes[t + 1]] = (-a).astype(BF16)
                elif k == 1:
                    x[low, lanes[t - 1]] = a.astype(BF16)
                else:
                    x[low, lanes[t]] = (pltpu.roll(a, 64, 1) * sign).astype(BF16)

        ghat = nn(tf[...], x[:, :wide])
        for t, (i, k) in enumerate(tiles):
            if k == 0:
                gr, gi = ghat[:, lanes[t]], ghat[:, lanes[t + 1]]
                wr, wi = what[0, i], what[1, i]
                pr = gr * wr - gi * wi
                pi = gr * wi + gi * wr
                pb[:E, lanes[t]] = pr.astype(BF16)
                pb[E:, lanes[t]] = (-pi).astype(BF16)
                pb[:E, lanes[t + 1]] = pi.astype(BF16)
                pb[E:, lanes[t + 1]] = pr.astype(BF16)
            elif k == 2:
                gm = ghat[:, lanes[t]]
                pm = gm * what[2, i] + pltpu.roll(gm, 64, 1) * what[3, i]
                pb[:E, lanes[t]] = pm.astype(BF16)
                pb[E:, lanes[t]] = (pltpu.roll(pm, 64, 1) * -sign).astype(BF16)
        fresh = nn(tb[...], pb[:, :wide])
        for q in range(PER_CHIP):
            for t in range(len(tiles)):
                m[mine][comb(t, q), :] = fresh[CHIPS * q : CHIPS * q + CHIPS, lanes[t]]
        spread(mine, bout[mine], bin[mine], BACK + mine)

    each(0, convolve)
    each(1, convolve)

    def second(e, slab):
        last = lf[e, 2].astype(BF16)
        sr = jnp.concatenate([lf[e, 0].astype(BF16), last[:, :64]], axis=1)
        si = jnp.concatenate([lf[e, 1].astype(BF16), last[:, 64:]], axis=1)
        new_ref[e, slab, 0] = sr
        new_ref[e, slab, 1] = si
        rr, ri = term(e, slab, 1, sr, si)
        ren_ref[e, slab, 0] = rr.astype(BF16)
        ren_ref[e, slab, 1] = ri.astype(BF16)

    for stage, slab in ((0, sl), (1, edge)):
        def give(mine):
            collect(mine, bout[mine], bin[mine], BACK + mine)
            for e in range(OWN):
                for t in range(len(SETS[mine])):
                    ns[mine][e, t] = m[mine][comb(t, OWN + e), :].astype(BF16)
                remote(ns[mine].at[e], nr[mine].at[e], NEW + OWN * mine + e, (sib, sl)).start()
            for e in range(OWN):
                for t, (i, k) in enumerate(SETS[mine]):
                    lf[e, k, pl.ds(i, CHIPS, stride=3), :] = m[mine][comb(t, e), :]

        def take(mine):
            other = 1 - mine
            for e in range(OWN):
                arrived(nr[other].at[e], NEW + OWN * other + e)
                for t, (i, k) in enumerate(SETS[other]):
                    lf[e, k, pl.ds(i, CHIPS, stride=3), :] = nr[other][e, t].astype(F32)

        each(stage, give)
        each(stage, take)
        for e in range(OWN):
            second(e, slab)

    for e in range(OWN):
        sent(hsend.at[e], HALO + e)
    for t in range(2):
        for e in range(OWN):
            sent(ls[t].at[e], LESSER + OWN * t + e)
            sent(ns[t].at[e], NEW + OWN * t + e)
        sent(out[t].at[pl.ds(0, CHIPS - 1)], THERE + t)
        sent(bout[t].at[pl.ds(0, CHIPS - 1)], BACK + t)


def shards(green_ret, sigma_less, screened):
    out = jax.ShapeDtypeStruct(sigma_less.shape, BF16)
    packed = pltpu.VMEM((OWN, B, 2 * B), BF16)

    def both(make):
        return [make(len(tiles)) for tiles in SETS]

    def tiles(n):
        return pltpu.VMEM((OWN, n, CHIPS, 128), BF16)

    def box(n):
        return pltpu.VMEM((CHIPS, n * PER_CHIP, 128), BF16)

    return pl.pallas_call(
        kernel,
        out_shape=(out, out),
        in_specs=[pl.BlockSpec(memory_space=pltpu.VMEM if n == 1 else pltpu.HBM) for n in range(6)],
        out_specs=[pl.BlockSpec(memory_space=pltpu.VMEM)] * 2,
        scratch_shapes=[
            pltpu.VMEM(green_ret.shape, BF16),
            pltpu.VMEM((2, 2, HALF, E), F32),
            pltpu.VMEM((2 * E, 2 * E), BF16),
            pltpu.VMEM((E, 2 * E), BF16),
            pltpu.VMEM((E, 2 * E), BF16),
            pltpu.VMEM((2, 2 * HALF, 2 * E), BF16),
            pltpu.VMEM((4, 3, E, 128), F32),
            packed, packed,
            pltpu.VMEM((OWN, 2, B, B), F32),
            pltpu.VMEM((OWN, 3, B, 128), F32),
            pltpu.VMEM((2 * E, 640), BF16),
            pltpu.VMEM((2 * E, 640), BF16),
            *[pltpu.VMEM((CHIPS * PITCH, 128), F32)] * 2,
            *both(tiles), *both(tiles), *both(box), *both(box), *both(box), *both(box), *both(tiles), *both(tiles),
            pltpu.SemaphoreType.DMA((5,)),
            pltpu.SemaphoreType.DMA((COPIES,)),
            pltpu.SemaphoreType.DMA((COPIES,)),
            pltpu.SemaphoreType.DMA((COPIES,)),
            pltpu.SemaphoreType.REGULAR((2,)),
        ],
        compiler_params=pltpu.CompilerParams(collective_id=0, has_side_effects=True, vmem_limit_bytes=50 * 2**20),
        name="wire",
    )(green_ret, sigma_less, jnp.transpose(screened, (1, 2, 3, 0)), *tables())


def solution(mesh):
    in_specs = (
        P("energy", "slab", None, None, None, None),
        P("energy", "slab", None, None, None),
        P(None, "slab", None, "energy"),
    )
    out_specs = (P("energy", "slab", None, None, None), P("energy", "slab", None, None, None))
    return jax.shard_map(shards, mesh=mesh, in_specs=in_specs, out_specs=out_specs, check_vma=False)
```

```python
import functools
import math

import jax
import jax.numpy as jnp
import numpy as np
from jax import lax
from jax.experimental import pallas as pl
from jax.experimental.pallas import tpu as pltpu
from jax.sharding import PartitionSpec as P

MESH = pl.DeviceIdType.MESH
F32, BF16 = jnp.float32, jnp.bfloat16
E, B = 384, 192
CHIPS, PER_CHIP, OWN = 64, 6, 3
PITCH = 32
SETS = (((0, 0), (0, 1), (0, 2), (1, 2)), ((1, 0), (1, 1), (2, 0), (2, 1), (2, 2)))
HALF = B * 3 // 2
HALO, LESSER, NEW, SCREEN, THERE, BACK, COPIES = 0, 3, 9, 15, 17, 19, 21
EARLY = 1
SCALE = 1.0 / (E * math.sqrt(E))


def tables():
    point = np.arange(E)

    def parts(rows, cols):
        angle = (rows[:, None] * cols[None, :] % E) * (2.0 * np.pi / E)
        return np.cos(angle), np.sin(angle)

    def held(core):
        own = [(OWN * core + q) % PER_CHIP for q in range(PER_CHIP)]
        return np.array([PER_CHIP * c + k for k in own for c in range(CHIPS)])

    cos, sin = parts(point, point)
    whole = np.concatenate([np.concatenate([cos, sin], 1), np.concatenate([-sin, cos], 1)], 0)
    there = np.stack([np.concatenate(parts(point, held(core)), 1) for core in range(2)])
    back = np.stack([np.concatenate(parts(held(core), point), 1) for core in range(2)])
    return [t.astype(np.float32).astype(BF16) for t in (whole, there, back)]


def nn(a, b):
    return lax.dot_general(a, b, (((1,), (0,)), ((), ())), preferred_element_type=F32)


def nt(a, b):
    return lax.dot_general(a, b, (((1,), (1,)), ((), ())), preferred_element_type=F32)


def adjoint_product(ar, ai, br, bi):
    return (nt(ar, br) + nt(ai, bi)).astype(BF16), (nt(ai, br) - nt(ar, bi)).astype(BF16)


def product(ar, ai, br, bi):
    return nn(ar, br) - nn(ai, bi), nn(ar, bi) + nn(ai, br)


def unpack(row):
    return (
        jnp.concatenate([row[:, :128], row[:, 256:320]], axis=1),
        jnp.concatenate([row[:, 128:256], row[:, 320:384]], axis=1),
    )


def comb(t, q):
    return pl.ds(t * PER_CHIP + q, CHIPS, stride=PITCH)


def kernel(
    g_hbm, s, w_hbm, tw_hbm, tf_hbm, tb_hbm, new_ref, ren_ref,
    g, w, tw, tf, tb, wall, what, hsend, hrecv, part, lf, x, pb,
    m0, m1, ls0, ls1, lr0, lr1, out0, out1, in0, in1, bout0, bout1, bin0, bin1, ns0, ns1, nr0, nr1,
    load, local, send, recv, line,
):
    me, sl = lax.axis_index("energy"), lax.axis_index("slab")
    chip, core = me // 2, me % 2
    py, pz, px = chip // 16, (chip // 4) % 4, chip % 4
    sib = me + 1 - 2 * core
    m, ls, lr, out, inn = (m0, m1), (ls0, ls1), (lr0, lr1), (out0, out1), (in0, in1)
    bout, bin, ns, nr = (bout0, bout1), (bin0, bin1), (ns0, ns1), (nr0, nr1)
    sign = jnp.where(lax.broadcasted_iota(jnp.int32, (1, 128), 1) < 64, 1.0, -1.0).astype(F32)

    def at(dy, dz, dx):
        return ((py + dy) % 4) * 16 + ((pz + dz) % 4) * 4 + (px + dx) % 4

    def signal(sem, device, slab):
        pl.semaphore_signal(sem, inc=1, device_id=(device, slab), device_id_type=MESH)

    barrier = pltpu.get_barrier_semaphore()
    signal(barrier, me, 1 - sl)
    signal(barrier, sib, sl)
    for d in range(1, 4):
        for off in ((0, 0, d), (d, 0, 0), (0, d, 0)):
            signal(barrier, 2 * at(*off) + core, sl)

    loads = [
        pltpu.make_async_copy(src, dst, load.at[n])
        for n, (src, dst) in enumerate(
            ((g_hbm, g), (w_hbm, w), (tw_hbm, tw), (tf_hbm.at[core], tf), (tb_hbm.at[core], tb))
        )
    ]
    for copy in loads:
        copy.start()

    def remote(src, dst, n, to):
        return pltpu.make_async_remote_copy(
            src_ref=src, dst_ref=dst, send_sem=send.at[n], recv_sem=recv.at[n], device_id=to, device_id_type=MESH
        )

    def arrived(dst, n):
        pltpu.make_async_copy(dst, dst, recv.at[n]).wait()

    def sent(src, n):
        pltpu.make_async_copy(src, src, send.at[n]).wait()

    def each(stage, do):
        for c in range(2):
            @pl.when(core == c)
            def _():
                do(c ^ stage)

    def spread(t, src, dst, n):
        rows = src.shape[1]

        def message(to):
            src[to] = m[t][pl.ds(pl.multiple_of(to * PITCH, 8), rows), :].astype(BF16)

        for dz in (2, 1, 3, 0):
            @pl.loop(0 if dz else 1, 16)
            def _(j):
                to = at(j // 4, dz, j + j // 4)
                message(to)
                remote(src.at[to], dst.at[chip], n, (2 * to + core, sl)).start()

        message(chip)
        pltpu.make_async_copy(src.at[chip], dst.at[chip], local.at[n]).start()

    def collect(t, src, dst, n):
        arrived(dst.at[pl.ds(0, CHIPS - 1)], n)
        pltpu.make_async_copy(src.at[chip], dst.at[chip], local.at[n]).wait()

        @pl.loop(0, CHIPS)
        def _(c):
            m[t][pl.ds(pl.multiple_of(c * PITCH, 8), dst.shape[1]), :] = dst[c].astype(F32)

    def pack(dst, re, im):
        dst[:, 0:128] = re[:, :128].astype(BF16)
        dst[:, 128:256] = im[:, :128].astype(BF16)
        dst[:, 256:320] = re[:, 128:].astype(BF16)
        dst[:, 320:384] = im[:, 128:].astype(BF16)

    edge = 1 - sl

    @pl.loop(0, OWN)
    def _(e):
        pack(hsend.at[e], s[e, edge, 0], s[e, edge, 1])

    pl.semaphore_wait(barrier, 11)
    halo = [remote(hsend.at[e], hrecv.at[e], HALO + e, (me, 1 - sl)) for e in range(OWN)]
    for copy in halo:
        copy.start()
    for d in range(1, 4):
        signal(line.at[0], 2 * at(0, 0, d) + core, sl)

    loads[1].wait()
    swap_w = []
    for slab in range(2):
        mine = wall.at[slab, pl.ds(pl.multiple_of(core * HALF, 32), HALF)]
        mine[:, :E] = w[slab, 0].astype(BF16)
        mine[:, E:] = w[slab, 1].astype(BF16)
        swap_w.append(remote(mine, mine, SCREEN + slab, (sib, sl)))
        swap_w[slab].start()
    pl.semaphore_wait(line.at[0], 3)
    for d in range(1, 4):
        signal(line.at[1], 2 * at(d, 0, 0) + core, sl)

    loads[0].wait()

    def term(e, slab, j, sr, si):
        gr, gi = g[e, slab, j, 0], g[e, slab, j, 1]
        ir, ii = adjoint_product(sr, si, gr, gi)
        return product(gr, gi, ir, ii)

    def inside(e, slab):
        lr, li = term(e, slab, 1, s[e, slab, 0], s[e, slab, 1])
        tr, ti = term(e, slab, 2 - 2 * slab, s[e, 1 - slab, 0], s[e, 1 - slab, 1])
        return lr + tr, li + ti

    def scatter(e, re, im):
        lf[e, 0] = re[:, :128]
        lf[e, 1] = im[:, :128]
        lf[e, 2, :, 0:64] = re[:, 128:]
        lf[e, 2, :, 64:128] = im[:, 128:]

    def deliver(stage, e):
        def do(mine):
            for t, (i, k) in enumerate(SETS[mine]):
                m[mine][comb(t, e), :] = lf[e, k, pl.ds(i, CHIPS, stride=3), :]
            other = 1 - mine
            for t, (i, k) in enumerate(SETS[other]):
                ls[other][e, t] = lf[e, k, pl.ds(i, CHIPS, stride=3), :].astype(BF16)
            remote(ls[other].at[e], lr[other].at[e], LESSER + OWN * other + e, (sib, sl)).start()

        each(stage, do)

    def receive(mine):
        for e in range(OWN):
            arrived(lr[mine].at[e], LESSER + OWN * mine + e)
            for t in range(len(SETS[mine])):
                m[mine][comb(t, OWN + e), :] = lr[mine][e, t].astype(F32)

    def send_there(mine):
        spread(mine, out[mine], inn[mine], THERE + mine)

    for e in range(OWN):
        scatter(e, *inside(e, sl))
        deliver(0, e)

    @pl.loop(0, OWN)
    def _(e):
        part[e, 0], part[e, 1] = inside(e, edge)

    pl.semaphore_wait(line.at[1], 3)

    for copy in swap_w:
        copy.wait()
    loads[2].wait()
    slab_of = ((sl + core) % 2, (sl + core + 1) % 2)

    def pairs(i, full):
        what[0, i] = full[:E, :128]
        what[1, i] = full[E:, :128]

    def tail(i, full):
        what[2, i, :, 0:64] = full[:E]
        what[2, i, :, 64:128] = full[:E]
        what[3, i, :, 0:64] = -full[E:]
        what[3, i, :, 64:128] = full[E:]

    def transform(c, lo, hi):
        return nt(tw[...], wall[slab_of[c], lo:hi, :]) * SCALE

    for c, i in ((0, 0), (1, 2)):
        full = transform(c, B * i, B * i + B)
        pairs(i, full)
        tail(i, full[:, 128:])
    pairs(1, transform(1, B, B + 128))
    tail(1, transform(0, B + 128, 2 * B))

    each(0, receive)
    for e in range(OWN):
        halo[e].wait()
        tr, ti = term(e, edge, 2 * edge, *unpack(hrecv[e]))
        scatter(e, part[e, 0] + tr, part[e, 1] + ti)
        deliver(1, e)
        if e == EARLY:
            each(0, send_there)

    each(1, receive)
    each(1, send_there)

    loads[3].wait()
    loads[4].wait()

    def convolve(mine):
        collect(mine, out[mine], inn[mine], THERE + mine)
        tiles = SETS[mine]
        wide = 128 * len(tiles)
        lanes = [slice(128 * t, 128 * t + 128) for t in range(len(tiles))]
        for q in range(PER_CHIP):
            top, low = slice(CHIPS * q, CHIPS * q + CHIPS), slice(E + CHIPS * q, E + CHIPS * q + CHIPS)
            for t, (i, k) in enumerate(tiles):
                a = m[mine][comb(t, q), :]
                x[top, lanes[t]] = a.astype(BF16)
                if k == 0:
                    x[low, lanes[t + 1]] = (-a).astype(BF16)
                elif k == 1:
                    x[low, lanes[t - 1]] = a.astype(BF16)
                else:
                    x[low, lanes[t]] = (pltpu.roll(a, 64, 1) * sign).astype(BF16)

        ghat = nn(tf[...], x[:, :wide])
        for t, (i, k) in enumerate(tiles):
            if k == 0:
                gr, gi = ghat[:, lanes[t]], ghat[:, lanes[t + 1]]
                wr, wi = what[0, i], what[1, i]
                pr = gr * wr - gi * wi
                pi = gr * wi + gi * wr
                pb[:E, lanes[t]] = pr.astype(BF16)
                pb[E:, lanes[t]] = (-pi).astype(BF16)
                pb[:E, lanes[t + 1]] = pi.astype(BF16)
                pb[E:, lanes[t + 1]] = pr.astype(BF16)
            elif k == 2:
                gm = ghat[:, lanes[t]]
                pm = gm * what[2, i] + pltpu.roll(gm, 64, 1) * what[3, i]
                pb[:E, lanes[t]] = pm.astype(BF16)
                pb[E:, lanes[t]] = (pltpu.roll(pm, 64, 1) * -sign).astype(BF16)
        fresh = nn(tb[...], pb[:, :wide])
        for q in range(PER_CHIP):
            for t in range(len(tiles)):
                m[mine][comb(t, q), :] = fresh[CHIPS * q : CHIPS * q + CHIPS, lanes[t]]
        spread(mine, bout[mine], bin[mine], BACK + mine)

    each(0, convolve)
    each(1, convolve)

    def second(e, slab):
        last = lf[e, 2].astype(BF16)
        sr = jnp.concatenate([lf[e, 0].astype(BF16), last[:, :64]], axis=1)
        si = jnp.concatenate([lf[e, 1].astype(BF16), last[:, 64:]], axis=1)
        new_ref[e, slab, 0] = sr
        new_ref[e, slab, 1] = si
        rr, ri = term(e, slab, 1, sr, si)
        ren_ref[e, slab, 0] = rr.astype(BF16)
        ren_ref[e, slab, 1] = ri.astype(BF16)

    for stage, slab in ((0, sl), (1, edge)):
        def give(mine):
            collect(mine, bout[mine], bin[mine], BACK + mine)
            for e in range(OWN):
                for t in range(len(SETS[mine])):
                    ns[mine][e, t] = m[mine][comb(t, OWN + e), :].astype(BF16)
                remote(ns[mine].at[e], nr[mine].at[e], NEW + OWN * mine + e, (sib, sl)).start()
            for e in range(OWN):
                for t, (i, k) in enumerate(SETS[mine]):
                    lf[e, k, pl.ds(i, CHIPS, stride=3), :] = m[mine][comb(t, e), :]

        each(stage, give)
        for e in range(OWN):
            def take(mine):
                other = 1 - mine
                arrived(nr[other].at[e], NEW + OWN * other + e)
                for t, (i, k) in enumerate(SETS[other]):
                    lf[e, k, pl.ds(i, CHIPS, stride=3), :] = nr[other][e, t].astype(F32)

            each(stage, take)
            second(e, slab)

    for t in range(2):
        for e in range(OWN):
            sent(ls[t].at[e], LESSER + OWN * t + e)
            sent(ns[t].at[e], NEW + OWN * t + e)
        sent(out[t].at[pl.ds(0, CHIPS - 1)], THERE + t)
        sent(bout[t].at[pl.ds(0, CHIPS - 1)], BACK + t)


def shards(green_ret, sigma_less, screened):
    out = jax.ShapeDtypeStruct(sigma_less.shape, BF16)
    packed = pltpu.VMEM((OWN, B, 2 * B), BF16)

    def both(make):
        return [make(len(tiles)) for tiles in SETS]

    def tiles(n):
        return pltpu.VMEM((OWN, n, CHIPS, 128), BF16)

    def box(n):
        return pltpu.VMEM((CHIPS, n * PER_CHIP, 128), BF16)

    return pl.pallas_call(
        kernel,
        out_shape=(out, out),
        in_specs=[pl.BlockSpec(memory_space=pltpu.VMEM if n == 1 else pltpu.HBM) for n in range(6)],
        out_specs=[pl.BlockSpec(memory_space=pltpu.VMEM)] * 2,
        scratch_shapes=[
            pltpu.VMEM(green_ret.shape, BF16),
            pltpu.VMEM((2, 2, HALF, E), F32),
            pltpu.VMEM((2 * E, 2 * E), BF16),
            pltpu.VMEM((E, 2 * E), BF16),
            pltpu.VMEM((E, 2 * E), BF16),
            pltpu.VMEM((2, 2 * HALF, 2 * E), BF16),
            pltpu.VMEM((4, 3, E, 128), F32),
            packed, packed,
            pltpu.VMEM((OWN, 2, B, B), F32),
            pltpu.VMEM((OWN, 3, B, 128), F32),
            pltpu.VMEM((2 * E, 640), BF16),
            pltpu.VMEM((2 * E, 640), BF16),
            *[pltpu.VMEM((CHIPS * PITCH, 128), F32)] * 2,
            *both(tiles), *both(tiles), *both(box), *both(box), *both(box), *both(box), *both(tiles), *both(tiles),
            pltpu.SemaphoreType.DMA((5,)),
            pltpu.SemaphoreType.DMA((COPIES,)),
            pltpu.SemaphoreType.DMA((COPIES,)),
            pltpu.SemaphoreType.DMA((COPIES,)),
            pltpu.SemaphoreType.REGULAR((2,)),
        ],
        compiler_params=pltpu.CompilerParams(collective_id=0, has_side_effects=True, vmem_limit_bytes=50 * 2**20),
        name="wire",
    )(green_ret, sigma_less, jnp.transpose(screened, (1, 2, 3, 0)), *tables())


def solution(mesh):
    in_specs = (
        P("energy", "slab", None, None, None, None),
        P("energy", "slab", None, None, None),
        P(None, "slab", None, "energy"),
    )
    out_specs = (P("energy", "slab", None, None, None), P("energy", "slab", None, None, None))
    return jax.shard_map(shards, mesh=mesh, in_specs=in_specs, out_specs=out_specs, check_vma=False)
```
